32 devices in a mesh: query: 4 (over x, core), bank: 8 (over z, y).
Axes of the slice: x: 2, y: 2, z: 4, core: 2. Of those that a mesh axis runs over, the one named last changes fastest.
Arguments:
- queries: bfloat16 [256, 32, 128], P(('query', 'bank'))
- passages: bfloat16 [2048, 128, 128], P('bank')
- passage_home: int32 [2048], replicated, may hold values from 0 to 2047, as said below
- candidates: int32 [256, 16], P(('query', 'bank')), may hold values from 0 to 2047, as said below
- positive: int32 [256], P(('query', 'bank')), may hold values from 0 to 15
Outputs:
- losses: float32 [256], P(('query', 'bank'))
- query_grads: float32 [256, 32, 128], P(('query', 'bank'))
The draws below stay inside these ranges and needn't reach their ends.
Inputs may be any that keep to these rules, and one draw needn't show every extreme that they name: `passage_home`: each passage id has its own storage row; storage row r lies on bank index r // 256. `candidates`: among the 128 list entries of one device's queries (aligned blocks of 8 queries, in order), at most 48 name passages stored on one bank index; in every block some bank index gets exactly 48, and in each group of 8 consecutive blocks it is the same bank index for all of them.
All inputs are finite; a program needn't handle non-finite values.
Results may differ from the reference program's by a relative error of at most 0.0049.
Values may be sent and summed in bfloat16 or wider, within the bound.
A program may use at most 128 MiB of HBM per device.

```python
import math
import jax
import jax.numpy as jnp
from jax import lax

DIM = 128
LQ = 32
LP = 128
K = 16
QD = 8
P_DEV = 256
NQ = 256
NP = 2048
CAP = 48


def pair_plan(key):
    shard_count = NP // P_DEV
    passage_home = jax.random.permutation(jax.random.fold_in(key, 101), NP).astype(jnp.int32)
    blocks = NQ // QD
    entries = QD * K
    groups = blocks // shard_count
    hottest = jax.random.randint(jax.random.fold_in(key, 102), (groups,), 0, shard_count)
    hot_block = jnp.repeat(hottest, shard_count)
    shifting = jax.random.randint(jax.random.fold_in(key, 103), (blocks, 1), 0, shard_count - 1)
    counter = jnp.arange(entries, dtype=jnp.int32)[None, :]
    spread = (hot_block[:, None] + 1 + (counter - CAP + shifting) % (shard_count - 1)) % shard_count
    owners = jnp.where(counter < CAP, hot_block[:, None], spread).astype(jnp.int32)
    shuffle_keys = jax.random.split(jax.random.fold_in(key, 104), blocks)
    owners = jax.vmap(lambda k, v: jax.random.permutation(k, v))(shuffle_keys, owners)
    local_slots = jax.random.randint(jax.random.fold_in(key, 105), (blocks, entries), 0, P_DEV)
    storage = owners * P_DEV + local_slots
    inverse = jnp.argsort(passage_home).astype(jnp.int32)
    return (passage_home, inverse[storage].reshape(NQ, K).astype(jnp.int32))


def passage_rows(key, storage):
    base_key = jax.random.fold_in(key, 201)

    def one_row(row):
        row_key = jax.random.fold_in(base_key, row)
        return jax.random.truncated_normal(row_key, -4.0, 4.0, (LP, DIM), jnp.float32)
    return jax.vmap(one_row)(storage)


def draw_passage_home(key, part):
    return pair_plan(key)[0]


def draw_candidates(key, part):
    return pair_plan(key)[1]


def draw_passages(key, part):
    return passage_rows(key, jnp.arange(NP, dtype=jnp.int32)).astype(jnp.bfloat16)


def draw_queries(key, part):
    return (0.18 * jax.random.truncated_normal(jax.random.fold_in(key, 301), -4.0, 4.0, (NQ, LQ, DIM), jnp.float32)).astype(jnp.bfloat16)


def touch_ends(array, stream_key, low, high):
    extent = array.shape
    place = [jax.random.randint(jax.random.fold_in(stream_key, axis), (), 0, extent[axis]) for axis in range(len(extent))]
    array = array.at[tuple(place)].set(low)
    longest = extent.index(max(extent))
    place[longest] = (place[longest] + 1) % extent[longest]
    return array.at[tuple(place)].set(high)


def setup_inputs(seed: int = 0) -> dict:
    key_of = jax.random.split(jax.random.key(seed), 6)
    return {
        "queries": draw_queries(jax.random.fold_in(key_of[5], 71), 0),
        "passages": draw_passages(jax.random.fold_in(key_of[5], 71), 0),
        "passage_home": draw_passage_home(jax.random.fold_in(key_of[5], 71), 0),
        "candidates": draw_candidates(jax.random.fold_in(key_of[5], 71), 0),
        "positive": touch_ends(jax.random.randint(key_of[4], (NQ,), 0, K), jax.random.fold_in(key_of[4], 1), 0, K - 1).astype(jnp.int32),
    }


def pair_terms(query_tok, passage_tiles):
    scores = jnp.einsum("nid,njd->nij", query_tok.astype(jnp.float32), passage_tiles.astype(jnp.float32))
    largest = jnp.max(scores, axis=2, keepdims=True)
    raised = jnp.exp(scores - largest)
    totals = jnp.sum(raised, axis=2, keepdims=True)
    maxima = largest[:, :, 0] + jnp.log(totals[:, :, 0])
    weights = (raised / totals).astype(jnp.bfloat16)
    token_basis = jnp.einsum("nij,njd->nid", weights.astype(jnp.float32), passage_tiles.astype(jnp.float32)).astype(jnp.bfloat16)
    return maxima, token_basis


def contrast(maxima, positive):
    similarity = jnp.sum(maxima, axis=2)
    largest = jnp.max(similarity, axis=1, keepdims=True)
    raised = jnp.exp(similarity - largest)
    totals = jnp.sum(raised, axis=1, keepdims=True)
    picked = jnp.arange(similarity.shape[1], dtype=jnp.int32)[None, :] == positive[:, None]
    losses = largest[:, 0] + jnp.log(totals[:, 0]) - jnp.sum(jnp.where(picked, similarity, jnp.zeros_like(similarity)), axis=1)
    coefficients = (raised / totals - picked.astype(similarity.dtype)).astype(jnp.bfloat16)
    return losses, coefficients


def reference(queries, passages, passage_home, candidates, positive):
    block_rows = math.gcd(NQ, 32)
    storage = passage_home[candidates]

    def one_block(block_index):
        first_row = (block_index * block_rows).astype(jnp.int32)
        query_part = lax.dynamic_slice_in_dim(queries, first_row, block_rows, 0)
        storage_part = lax.dynamic_slice_in_dim(storage, first_row, block_rows, 0)
        positive_part = lax.dynamic_slice_in_dim(positive, first_row, block_rows, 0)
        passage_tiles = passages[storage_part.reshape(-1)]
        paired = jnp.repeat(query_part, K, axis=0)
        maxima, token_basis = pair_terms(paired, passage_tiles)
        losses, coefficients = contrast(maxima.reshape(block_rows, K, LQ), positive_part)
        gradient = jnp.einsum("qk,qkd->qd", coefficients.astype(jnp.float32), token_basis.reshape(block_rows, K, LQ * DIM).astype(jnp.float32))
        return losses, gradient.reshape(block_rows, LQ, DIM)

    losses, gradient = lax.map(one_block, jnp.arange(NQ // block_rows, dtype=jnp.int32))
    return losses.reshape(NQ), gradient.reshape(NQ, LQ, DIM)
```

```python
import jax
import jax.numpy as jnp
from jax import lax
from jax.experimental import pallas as pl
from jax.experimental.pallas import tpu as pltpu
from jax.sharding import PartitionSpec as P

GROUP = 8


def pair_kernel(row_ref, qid_ref, queries_ref, passages_ref, basis_ref, sim_ref):
    slots = row_ref.shape[0]

    @pl.loop(0, slots // GROUP)
    def _(group):
        first = group * GROUP
        tiles = [passages_ref[row_ref[first + u]] for u in range(GROUP)]
        scores = [
            lax.dot_general(
                queries_ref[qid_ref[first + u]],
                tiles[u],
                (((1,), (1,)), ((), ())),
                preferred_element_type=jnp.float32,
            )
            for u in range(GROUP)
        ]
        largest = [jnp.max(s, axis=1, keepdims=True) for s in scores]
        raised = [jnp.exp(s - m) for s, m in zip(scores, largest)]
        totals = [jnp.sum(r, axis=1, keepdims=True) for r in raised]
        weights = [(r / t).astype(jnp.bfloat16) for r, t in zip(raised, totals)]
        for u in range(GROUP):
            basis_ref[first + u] = jnp.dot(
                weights[u], tiles[u], preferred_element_type=jnp.float32
            ).astype(jnp.bfloat16)
        rows = [
            jnp.sum(m + jnp.log(t), axis=0, keepdims=True) for m, t in zip(largest, totals)
        ]
        sim_ref[pl.ds(pl.multiple_of(first, GROUP), GROUP), :] = jnp.broadcast_to(
            jnp.concatenate(rows, axis=0), (GROUP, sim_ref.shape[1])
        )


def pair_terms(rows, qids, queries, passages):
    slots = rows.shape[0]
    query_len, feature_dim = queries.shape[1:]
    return pl.pallas_call(
        pair_kernel,
        out_shape=(
            jax.ShapeDtypeStruct((slots, query_len, feature_dim), jnp.bfloat16),
            jax.ShapeDtypeStruct((slots, 128), jnp.float32),
        ),
        in_specs=[pl.BlockSpec(memory_space=pltpu.SMEM)] * 2
        + [pl.BlockSpec(memory_space=pltpu.VMEM)] * 2,
        out_specs=(pl.BlockSpec(memory_space=pltpu.VMEM),) * 2,
        compiler_params=pltpu.CompilerParams(vmem_limit_bytes=40 * 1024 * 1024),
    )(rows, qids, queries, passages)


def slot_list(storage, positive, holdings, capacity):
    count, listed = storage.shape
    me = lax.axis_index("bank")
    owned = (storage // holdings == me).reshape(-1)
    entry = jnp.arange(count * listed, dtype=jnp.int32)
    picked = (jnp.arange(listed, dtype=jnp.int32)[None, :] == positive[:, None]).astype(jnp.int32)
    code = (entry * 2 + picked.reshape(-1)) * holdings + (storage % holdings).reshape(-1)
    position = jnp.cumsum(owned.astype(jnp.int32)) - 1
    target = jnp.where(owned, position, capacity)
    table = jnp.full((capacity,), -1, jnp.int32).at[target].set(code, mode="drop")
    valid = table >= 0
    table = jnp.maximum(table, 0)
    rows = table % holdings
    rest = table // holdings
    return rows, rest // 2 // listed, valid, rest % 2


def body(queries, passages, passage_home, candidates, positive):
    shards = lax.axis_size("bank")
    query_rows, query_len, feature_dim = queries.shape
    listed = candidates.shape[1]
    holdings = passages.shape[0]
    entries = query_rows * listed
    capacity = 3 * entries
    group = shards * query_rows
    info = jnp.concatenate([passage_home[candidates], positive[:, None]], axis=1)
    infos = lax.all_gather(info, "bank", axis=0, tiled=True)
    all_queries = lax.all_gather(queries, "bank", axis=0, tiled=True)
    rows, qids, valid, picked = slot_list(infos[:, :listed], infos[:, listed], holdings, capacity)
    basis, sims = pair_terms(rows, qids, all_queries, passages)
    match = (qids[None, :] == jnp.arange(group, dtype=jnp.int32)[:, None]) & valid[None, :]
    chosen = match & (picked[None, :] > 0)
    table = jnp.where(match, sims[:, 0][None, :], -jnp.inf)
    largest = jnp.max(table, axis=1)
    safe = jnp.where(largest == -jnp.inf, 0.0, largest)
    partial = jnp.sum(jnp.exp(table - safe[:, None]), axis=1)
    wanted = jnp.sum(jnp.where(chosen, table, 0.0), axis=1)
    stats = lax.all_gather(jnp.stack([largest, partial, wanted]), "bank", axis=0, tiled=False)
    top = jnp.max(stats[:, 0], axis=0)
    total = jnp.sum(stats[:, 1] * jnp.exp(stats[:, 0] - top[None, :]), axis=0)
    losses = top + jnp.log(total) - jnp.sum(stats[:, 2], axis=0)
    mine = lax.axis_index("bank") * query_rows
    losses = lax.dynamic_slice_in_dim(losses, mine, query_rows, 0)
    shares = jnp.exp(table - top[:, None]) / total[:, None]
    coefficients = (shares - chosen.astype(jnp.float32)).astype(jnp.bfloat16)
    part = jnp.dot(
        coefficients,
        basis.reshape(capacity, query_len * feature_dim),
        preferred_element_type=jnp.float32,
    ).astype(jnp.bfloat16)
    parts = lax.all_to_all(
        part.reshape(shards, query_rows, query_len * feature_dim), "bank", 0, 0, tiled=True
    )
    gradient = jnp.sum(parts.astype(jnp.float32), axis=0)
    return (losses, gradient.reshape(query_rows, query_len, feature_dim))


def solution(mesh):
    return jax.shard_map(
        body,
        mesh=mesh,
        in_specs=(
            P(("query", "bank"), None, None),
            P("bank", None, None),
            P(),
            P(("query", "bank"), None),
            P(("query", "bank")),
        ),
        out_specs=(P(("query", "bank")), P(("query", "bank"), None, None)),
        check_vma=False,
    )
```

```python
import functools

import jax
import jax.numpy as jnp
from jax import lax
from jax.experimental import pallas as pl
from jax.experimental.pallas import tpu as pltpu
from jax.sharding import PartitionSpec as P

GROUP = 8


MESH = pl.DeviceIdType.MESH


def quarter_sum(x):
    n = x.shape[0] // 4
    return (x[:n] + x[n : 2 * n]) + (x[2 * n : 3 * n] + x[3 * n :])


def quarter_product(x):
    n = x.shape[0] // 4
    return (x[:n] * x[n : 2 * n]) * (x[2 * n : 3 * n] * x[3 * n :])


def pair_kernel(row_ref, qid_ref, queries_ref, passages_ref, basis_ref, sim_ref):
    slots = row_ref.shape[0]

    @pl.loop(0, slots // GROUP)
    def _(group):
        first = group * GROUP
        tiles = [passages_ref[row_ref[first + u]] for u in range(GROUP)]
        scores = [
            lax.dot_general(
                queries_ref[qid_ref[first + u]],
                tiles[u],
                (((1,), (1,)), ((), ())),
                preferred_element_type=jnp.float32,
            )
            for u in range(GROUP)
        ]
        largest = [jnp.max(s, axis=1, keepdims=True) for s in scores]
        raised = [jnp.exp(s - m) for s, m in zip(scores, largest)]
        totals = [jnp.sum(r, axis=1, keepdims=True) for r in raised]
        guesses = [pl.reciprocal(t, approx=True) for t in totals]
        inverse = [g * (2.0 - t * g) for g, t in zip(guesses, totals)]
        weights = [(r * v).astype(jnp.bfloat16) for r, v in zip(raised, inverse)]
        for u in range(GROUP):
            basis_ref[first + u] = jnp.dot(
                weights[u], tiles[u], preferred_element_type=jnp.float32
            ).astype(jnp.bfloat16)
        rows = [
            jnp.sum(quarter_sum(m) + jnp.log(quarter_product(t)), axis=0, keepdims=True)
            for m, t in zip(largest, totals)
        ]
        sim_ref[pl.ds(pl.multiple_of(first, GROUP), GROUP), :] = jnp.broadcast_to(
            jnp.concatenate(rows, axis=0), (GROUP, sim_ref.shape[1])
        )


def pair_terms(rows, qids, queries, passages):
    slots = rows.shape[0]
    query_len, feature_dim = queries.shape[1:]
    return pl.pallas_call(
        pair_kernel,
        out_shape=(
            jax.ShapeDtypeStruct((slots, query_len, feature_dim), jnp.bfloat16),
            jax.ShapeDtypeStruct((slots, 128), jnp.float32),
        ),
        in_specs=[pl.BlockSpec(memory_space=pltpu.SMEM)] * 2
        + [pl.BlockSpec(memory_space=pltpu.VMEM)] * 2,
        out_specs=(pl.BlockSpec(memory_space=pltpu.VMEM),) * 2,
        compiler_params=pltpu.CompilerParams(vmem_limit_bytes=40 * 1024 * 1024),
    )(rows, qids, queries, passages)


def greet(shards, me):
    barrier = pltpu.get_barrier_semaphore()
    for step in range(1, shards):
        pl.semaphore_signal(
            barrier, inc=1, device_id={"bank": lax.rem(me + step, shards)}, device_id_type=MESH
        )
    pl.semaphore_wait(barrier, shards - 1)


def gather_kernel(shards, inner, q_ref, info_ref, all_q_ref, all_info_ref, sends, recvs, isends, irecvs):
    outer = shards // inner
    me = lax.axis_index("bank")
    z, y = me // inner, lax.rem(me, inner)
    rows = q_ref.shape[0]

    def place(index):
        return pl.ds(pl.multiple_of(index * rows, rows), rows)

    def peer(dz, dy):
        return lax.rem(z + dz, outer) * inner + lax.rem(y + dy, inner)

    def send(src, block, slot, target):
        copy = pltpu.make_async_remote_copy(
            src_ref=src,
            dst_ref=all_q_ref.at[place(block)],
            send_sem=sends.at[slot],
            recv_sem=recvs.at[slot],
            device_id={"bank": target},
            device_id_type=MESH,
        )
        copy.start()
        return copy

    greet(shards, me)
    copies = {}
    for dz in range(1, outer):
        copies[dz * inner] = send(q_ref, me, dz * inner, peer(dz, 0))
    small = []
    for step in range(1, shards):
        copy = pltpu.make_async_remote_copy(
            src_ref=info_ref,
            dst_ref=all_info_ref.at[place(me)],
            send_sem=isends.at[step],
            recv_sem=irecvs.at[step],
            device_id={"bank": lax.rem(me + step, shards)},
            device_id_type=MESH,
        )
        copy.start()
        small.append(copy)
    for dy in range(1, inner):
        copies[dy] = send(q_ref, me, dy, peer(0, dy))
    all_q_ref[place(me)] = q_ref[...]
    all_info_ref[place(me)] = info_ref[...]
    for dz in range(1, outer):
        copies[dz * inner].wait_recv()
        source = lax.rem(z + outer - dz, outer) * inner + y
        for dy in range(1, inner):
            copies[dz * inner + dy] = send(
                all_q_ref.at[place(source)], source, dz * inner + dy, peer(0, dy)
            )
    for slot, copy in copies.items():
        if slot < inner or slot % inner:
            copy.wait_recv()
        copy.wait_send()
    for copy in small:
        copy.wait()


def gather_queries(queries, info):
    shards = lax.axis_size("bank")
    inner = 1
    while (2 * inner) ** 2 <= shards:
        inner *= 2
    vmem = pl.BlockSpec(memory_space=pltpu.VMEM)
    return pl.pallas_call(
        functools.partial(gather_kernel, shards, inner),
        out_shape=(
            jax.ShapeDtypeStruct((shards * queries.shape[0],) + queries.shape[1:], queries.dtype),
            jax.ShapeDtypeStruct((shards * info.shape[0], info.shape[1]), info.dtype),
        ),
        in_specs=[vmem, vmem],
        out_specs=(vmem, vmem),
        scratch_shapes=[pltpu.SemaphoreType.DMA((shards,))] * 4,
        compiler_params=pltpu.CompilerParams(
            collective_id=0, has_side_effects=True, vmem_limit_bytes=16 * 1024 * 1024
        ),
    )(queries, info)


def contrast_kernel(shards, sim_ref, meta_ref, coef_ref, loss_ref, slots, sends, recvs):
    me = lax.axis_index("bank")
    width = coef_ref.shape[1]
    capacity = sim_ref.shape[0]
    meta = meta_ref[...]
    lane = lax.broadcasted_iota(jnp.int32, (capacity, width), 1)
    chosen = meta == lane * 2 + 1
    match = chosen | (meta == lane * 2)
    table = jnp.where(match, sim_ref[:, :1], -jnp.inf)
    largest = jnp.max(table, axis=0, keepdims=True)
    safe = jnp.where(largest == -jnp.inf, 0.0, largest)
    partial = jnp.sum(jnp.exp(table - safe), axis=0, keepdims=True)
    wanted = jnp.sum(jnp.where(chosen, table, 0.0), axis=0, keepdims=True)
    slots[me] = jnp.concatenate([largest, partial, wanted, jnp.zeros((5, width), jnp.float32)], axis=0)
    greet(shards, me)
    copies = []
    for step in range(1, shards):
        copy = pltpu.make_async_remote_copy(
            src_ref=slots.at[me],
            dst_ref=slots.at[me],
            send_sem=sends.at[step],
            recv_sem=recvs.at[step],
            device_id={"bank": lax.rem(me + step, shards)},
            device_id_type=MESH,
        )
        copy.start()
        copies.append(copy)
    for copy in copies:
        copy.wait()
    tops = [slots[b, 0:1, :] for b in range(shards)]
    top = functools.reduce(jnp.maximum, tops)
    top = jnp.where(top == -jnp.inf, 0.0, top)
    total = sum(slots[b, 1:2, :] * jnp.exp(tops[b] - top) for b in range(shards))
    picked = sum(slots[b, 2:3, :] for b in range(shards))
    loss_ref[...] = jnp.broadcast_to(top + jnp.log(total) - picked, loss_ref.shape)
    total = jnp.where(total == 0.0, 1.0, total)
    shares = jnp.exp(table - top) / total
    coef_ref[...] = (shares - jnp.where(chosen, 1.0, 0.0)).astype(coef_ref.dtype)


def contrast(sims, meta, group):
    shards = lax.axis_size("bank")
    width = -(-group // 128) * 128
    vmem = pl.BlockSpec(memory_space=pltpu.VMEM)
    return pl.pallas_call(
        functools.partial(contrast_kernel, shards),
        out_shape=(
            jax.ShapeDtypeStruct((sims.shape[0], width), jnp.bfloat16),
            jax.ShapeDtypeStruct((8, width), jnp.float32),
        ),
        in_specs=[vmem, vmem],
        out_specs=(vmem, vmem),
        scratch_shapes=[
            pltpu.VMEM((shards, 8, width), jnp.float32),
            pltpu.SemaphoreType.DMA((shards,)),
            pltpu.SemaphoreType.DMA((shards,)),
        ],
        compiler_params=pltpu.CompilerParams(
            collective_id=1, has_side_effects=True, vmem_limit_bytes=16 * 1024 * 1024
        ),
    )(sims, meta)


def slot_list(storage, positive, holdings, capacity):
    count, listed = storage.shape
    me = lax.axis_index("bank")
    owned = (storage // holdings == me).reshape(-1)
    entry = jnp.arange(count * listed, dtype=jnp.int32)
    picked = (jnp.arange(listed, dtype=jnp.int32)[None, :] == positive[:, None]).astype(jnp.int32)
    query = entry // listed
    code = (query * 2 + picked.reshape(-1)) * holdings + (storage % holdings).reshape(-1)
    position = jnp.cumsum(owned.astype(jnp.int32)) - 1
    target = jnp.where(owned, position, -1)
    here = target[None, :] == jnp.arange(capacity, dtype=jnp.int32)[:, None]
    table = jnp.sum(jnp.where(here, code[None, :] + 1, 0), axis=1) - 1
    meta = jnp.where(table >= 0, table // holdings, -1)
    table = jnp.maximum(table, 0)
    return table % holdings, table // holdings // 2, meta


def body(queries, passages, passage_home, candidates, positive):
    shards = lax.axis_size("bank")
    query_rows, query_len, feature_dim = queries.shape
    listed = candidates.shape[1]
    holdings = passages.shape[0]
    capacity = 3 * query_rows * listed
    group = shards * query_rows
    info = jnp.concatenate([passage_home[candidates], positive[:, None]], axis=1)
    info = jnp.pad(info, ((0, 0), (0, 128 - info.shape[1])))
    all_queries, infos = gather_queries(queries, info)
    rows, qids, meta = slot_list(infos[:, :listed], infos[:, listed], holdings, capacity)
    basis, sims = pair_terms(rows, qids, all_queries, passages)
    coefficients, losses = contrast(sims, meta[:, None], group)
    mine = lax.axis_index("bank") * query_rows
    losses = lax.dynamic_slice_in_dim(losses[0], mine, query_rows, 0)
    part = lax.dot_general(
        coefficients[:, :group],
        basis.reshape(capacity, query_len * feature_dim),
        (((0,), (0,)), ((), ())),
        preferred_element_type=jnp.float32,
    ).astype(jnp.bfloat16)
    parts = lax.all_to_all(
        part.reshape(shards, query_rows, query_len * feature_dim), "bank", 0, 0, tiled=True
    )
    gradient = jnp.sum(parts.astype(jnp.float32), axis=0)
    return (losses, gradient.reshape(query_rows, query_len, feature_dim))


def solution(mesh):
    return jax.shard_map(
        body,
        mesh=mesh,
        in_specs=(
            P(("query", "bank"), None, None),
            P("bank", None, None),
            P(),
            P(("query", "bank"), None),
            P(("query", "bank")),
        ),
        out_specs=(P(("query", "bank")), P(("query", "bank"), None, None)),
        check_vma=False,
    )
```

```python
import functools

import jax
import jax.numpy as jnp
from jax import lax
from jax.experimental import pallas as pl
from jax.experimental.pallas import tpu as pltpu
from jax.sharding import PartitionSpec as P

GROUP = 32


MESH = pl.DeviceIdType.MESH


def quarter_sum(x):
    n = x.shape[0] // 4
    return (x[:n] + x[n : 2 * n]) + (x[2 * n : 3 * n] + x[3 * n :])


def quarter_product(x):
    n = x.shape[0] // 4
    return (x[:n] * x[n : 2 * n]) * (x[2 * n : 3 * n] * x[3 * n :])


def pair_kernel(row_ref, qid_ref, queries_ref, passages_ref, basis_ref, sim_ref, held, arrived):
    groups = row_ref.shape[0] // GROUP

    def fetch(group, u):
        half = lax.rem(group, 2)
        return pltpu.make_async_copy(
            passages_ref.at[row_ref[group * GROUP + u]], held.at[half, u], arrived.at[half, u]
        )

    for u in range(GROUP):
        fetch(0, u).start()

    @pl.loop(0, groups)
    def _(group):
        first = group * GROUP

        @pl.when(group + 1 < groups)
        def _():
            for u in range(GROUP):
                fetch(group + 1, u).start()

        for u in range(GROUP):
            fetch(group, u).wait()
        half = lax.rem(group, 2)
        tiles = [held[half, u] for u in range(GROUP)]
        scores = [
            lax.dot_general(
                queries_ref[qid_ref[first + u]],
                tiles[u],
                (((1,), (1,)), ((), ())),
                preferred_element_type=jnp.float32,
            )
            for u in range(GROUP)
        ]
        largest = [jnp.max(s, axis=1, keepdims=True) for s in scores]
        raised = [jnp.exp(s - m) for s, m in zip(scores, largest)]
        totals = [jnp.sum(r, axis=1, keepdims=True) for r in raised]
        guesses = [pl.reciprocal(t, approx=True) for t in totals]
        inverse = [g * (2.0 - t * g) for g, t in zip(guesses, totals)]
        weights = [(r * v).astype(jnp.bfloat16) for r, v in zip(raised, inverse)]
        for u in range(GROUP):
            basis_ref[first + u] = jnp.dot(
                weights[u], tiles[u], preferred_element_type=jnp.float32
            ).astype(jnp.bfloat16)
        rows = [
            jnp.sum(quarter_sum(m) + jnp.log(quarter_product(t)), axis=0, keepdims=True)
            for m, t in zip(largest, totals)
        ]
        sim_ref[pl.ds(pl.multiple_of(first, GROUP), GROUP), :] = jnp.broadcast_to(
            jnp.concatenate(rows, axis=0), (GROUP, sim_ref.shape[1])
        )


def pair_terms(rows, qids, queries, passages):
    slots = rows.shape[0]
    query_len, feature_dim = queries.shape[1:]
    return pl.pallas_call(
        pair_kernel,
        out_shape=(
            jax.ShapeDtypeStruct((slots, query_len, feature_dim), jnp.bfloat16),
            jax.ShapeDtypeStruct((slots, 128), jnp.float32),
        ),
        in_specs=[pl.BlockSpec(memory_space=pltpu.SMEM)] * 2
        + [pl.BlockSpec(memory_space=pltpu.VMEM), pl.BlockSpec(memory_space=pltpu.HBM)],
        out_specs=(pl.BlockSpec(memory_space=pltpu.VMEM),) * 2,
        scratch_shapes=[
            pltpu.VMEM((2, GROUP) + passages.shape[1:], passages.dtype),
            pltpu.SemaphoreType.DMA((2, GROUP)),
        ],
        compiler_params=pltpu.CompilerParams(vmem_limit_bytes=57 * 1024 * 1024),
    )(rows, qids, queries, passages)


def greet(shards, me):
    barrier = pltpu.get_barrier_semaphore()
    for step in range(1, shards):
        pl.semaphore_signal(
            barrier, inc=1, device_id={"bank": lax.rem(me + step, shards)}, device_id_type=MESH
        )
    pl.semaphore_wait(barrier, shards - 1)


def gather_kernel(shards, inner, q_ref, info_ref, all_q_ref, all_info_ref, sends, recvs, isends, irecvs):
    outer = shards // inner
    me = lax.axis_index("bank")
    z, y = me // inner, lax.rem(me, inner)
    rows = q_ref.shape[0]

    def place(index):
        return pl.ds(pl.multiple_of(index * rows, rows), rows)

    def peer(dz, dy):
        return lax.rem(z + dz, outer) * inner + lax.rem(y + dy, inner)

    def send(src, block, slot, target):
        copy = pltpu.make_async_remote_copy(
            src_ref=src,
            dst_ref=all_q_ref.at[place(block)],
            send_sem=sends.at[slot],
            recv_sem=recvs.at[slot],
            device_id={"bank": target},
            device_id_type=MESH,
        )
        copy.start()
        return copy

    greet(shards, me)
    copies = {}
    for dz in range(1, outer):
        copies[dz * inner] = send(q_ref, me, dz * inner, peer(dz, 0))
    small = []
    for step in range(1, shards):
        copy = pltpu.make_async_remote_copy(
            src_ref=info_ref,
            dst_ref=all_info_ref.at[place(me)],
            send_sem=isends.at[step],
            recv_sem=irecvs.at[step],
            device_id={"bank": lax.rem(me + step, shards)},
            device_id_type=MESH,
        )
        copy.start()
        small.append(copy)
    for dy in range(1, inner):
        copies[dy] = send(q_ref, me, dy, peer(0, dy))
    all_q_ref[place(me)] = q_ref[...]
    all_info_ref[place(me)] = info_ref[...]
    for dz in range(1, outer):
        copies[dz * inner].wait_recv()
        source = lax.rem(z + outer - dz, outer) * inner + y
        for dy in range(1, inner):
            copies[dz * inner + dy] = send(
                all_q_ref.at[place(source)], source, dz * inner + dy, peer(0, dy)
            )
    for slot, copy in copies.items():
        if slot < inner or slot % inner:
            copy.wait_recv()
        copy.wait_send()
    for copy in small:
        copy.wait()


def gather_queries(queries, info):
    shards = lax.axis_size("bank")
    inner = 1
    while (2 * inner) ** 2 <= shards:
        inner *= 2
    vmem = pl.BlockSpec(memory_space=pltpu.VMEM)
    return pl.pallas_call(
        functools.partial(gather_kernel, shards, inner),
        out_shape=(
            jax.ShapeDtypeStruct((shards * queries.shape[0],) + queries.shape[1:], queries.dtype),
            jax.ShapeDtypeStruct((shards * info.shape[0], info.shape[1]), info.dtype),
        ),
        in_specs=[vmem, vmem],
        out_specs=(vmem, vmem),
        scratch_shapes=[pltpu.SemaphoreType.DMA((shards,))] * 4,
        compiler_params=pltpu.CompilerParams(
            collective_id=0, has_side_effects=True, vmem_limit_bytes=16 * 1024 * 1024
        ),
    )(queries, info)


def contrast_kernel(shards, sim_ref, meta_ref, coef_ref, loss_ref, slots, sends, recvs):
    me = lax.axis_index("bank")
    width = coef_ref.shape[1]
    capacity = sim_ref.shape[0]
    meta = meta_ref[...]
    lane = lax.broadcasted_iota(jnp.int32, (capacity, width), 1)
    chosen = meta == lane * 2 + 1
    match = chosen | (meta == lane * 2)
    table = jnp.where(match, sim_ref[:, :1], -jnp.inf)
    largest = jnp.max(table, axis=0, keepdims=True)
    safe = jnp.where(largest == -jnp.inf, 0.0, largest)
    partial = jnp.sum(jnp.exp(table - safe), axis=0, keepdims=True)
    wanted = jnp.sum(jnp.where(chosen, table, 0.0), axis=0, keepdims=True)
    slots[me] = jnp.concatenate([largest, partial, wanted, jnp.zeros((5, width), jnp.float32)], axis=0)
    greet(shards, me)
    copies = []
    for step in range(1, shards):
        copy = pltpu.make_async_remote_copy(
            src_ref=slots.at[me],
            dst_ref=slots.at[me],
            send_sem=sends.at[step],
            recv_sem=recvs.at[step],
            device_id={"bank": lax.rem(me + step, shards)},
            device_id_type=MESH,
        )
        copy.start()
        copies.append(copy)
    for copy in copies:
        copy.wait()
    tops = [slots[b, 0:1, :] for b in range(shards)]
    top = functools.reduce(jnp.maximum, tops)
    top = jnp.where(top == -jnp.inf, 0.0, top)
    total = sum(slots[b, 1:2, :] * jnp.exp(tops[b] - top) for b in range(shards))
    picked = sum(slots[b, 2:3, :] for b in range(shards))
    loss_ref[...] = jnp.broadcast_to(top + jnp.log(total) - picked, loss_ref.shape)
    total = jnp.where(total == 0.0, 1.0, total)
    shares = jnp.exp(table - top) / total
    coef_ref[...] = (shares - jnp.where(chosen, 1.0, 0.0)).astype(coef_ref.dtype)


def contrast(sims, meta, group):
    shards = lax.axis_size("bank")
    width = -(-group // 128) * 128
    vmem = pl.BlockSpec(memory_space=pltpu.VMEM)
    return pl.pallas_call(
        functools.partial(contrast_kernel, shards),
        out_shape=(
            jax.ShapeDtypeStruct((sims.shape[0], width), jnp.bfloat16),
            jax.ShapeDtypeStruct((8, width), jnp.float32),
        ),
        in_specs=[vmem, vmem],
        out_specs=(vmem, vmem),
        scratch_shapes=[
            pltpu.VMEM((shards, 8, width), jnp.float32),
            pltpu.SemaphoreType.DMA((shards,)),
            pltpu.SemaphoreType.DMA((shards,)),
        ],
        compiler_params=pltpu.CompilerParams(
            collective_id=1, has_side_effects=True, vmem_limit_bytes=16 * 1024 * 1024
        ),
    )(sims, meta)


def slot_list(storage, positive, holdings, capacity):
    count, listed = storage.shape
    me = lax.axis_index("bank")
    owned = (storage // holdings == me).reshape(-1)
    entry = jnp.arange(count * listed, dtype=jnp.int32)
    picked = (jnp.arange(listed, dtype=jnp.int32)[None, :] == positive[:, None]).astype(jnp.int32)
    query = entry // listed
    code = (query * 2 + picked.reshape(-1)) * holdings + (storage % holdings).reshape(-1)
    position = jnp.cumsum(owned.astype(jnp.int32)) - 1
    target = jnp.where(owned, position, -1)
    here = target[None, :] == jnp.arange(capacity, dtype=jnp.int32)[:, None]
    table = jnp.sum(jnp.where(here, code[None, :] + 1, 0), axis=1) - 1
    meta = jnp.where(table >= 0, table // holdings, -1)
    table = jnp.maximum(table, 0)
    return table % holdings, table // holdings // 2, meta


def body(queries, passages, passage_home, candidates, positive):
    shards = lax.axis_size("bank")
    query_rows, query_len, feature_dim = queries.shape
    listed = candidates.shape[1]
    holdings = passages.shape[0]
    capacity = 3 * query_rows * listed
    group = shards * query_rows
    info = jnp.concatenate([passage_home[candidates], positive[:, None]], axis=1)
    info = jnp.pad(info, ((0, 0), (0, 128 - info.shape[1])))
    all_queries, infos = gather_queries(queries, info)
    rows, qids, meta = slot_list(infos[:, :listed], infos[:, listed], holdings, capacity)
    basis, sims = pair_terms(rows, qids, all_queries, passages)
    coefficients, losses = contrast(sims, meta[:, None], group)
    mine = lax.axis_index("bank") * query_rows
    losses = lax.dynamic_slice_in_dim(losses[0], mine, query_rows, 0)
    part = lax.dot_general(
        coefficients[:, :group],
        basis.reshape(capacity, query_len * feature_dim),
        (((0,), (0,)), ((), ())),
        preferred_element_type=jnp.float32,
    ).astype(jnp.bfloat16)
    parts = lax.all_to_all(
        part.reshape(shards, query_rows, query_len * feature_dim), "bank", 0, 0, tiled=True
    )
    gradient = jnp.sum(parts.astype(jnp.float32), axis=0)
    return (losses, gradient.reshape(query_rows, query_len, feature_dim))


def solution(mesh):
    return jax.shard_map(
        body,
        mesh=mesh,
        in_specs=(
            P(("query", "bank"), None, None),
            P("bank", None, None),
            P(),
            P(("query", "bank"), None),
            P(("query", "bank")),
        ),
        out_specs=(P(("query", "bank")), P(("query", "bank"), None, None)),
        check_vma=False,
    )
```

```python
import functools

import jax
import jax.numpy as jnp
from jax import lax
from jax.experimental import pallas as pl
from jax.experimental.pallas import tpu as pltpu
from jax.sharding import PartitionSpec as P

GROUP = 32


MESH = pl.DeviceIdType.MESH


def quarter_sum(x):
    n = x.shape[0] // 4
    return (x[:n] + x[n : 2 * n]) + (x[2 * n : 3 * n] + x[3 * n :])


def quarter_product(x):
    n = x.shape[0] // 4
    return (x[:n] * x[n : 2 * n]) * (x[2 * n : 3 * n] * x[3 * n :])


def pair_kernel(row_ref, qid_ref, queries_ref, passages_ref, basis_ref, sim_ref, held, arrived):
    groups = row_ref.shape[0] // GROUP
    query_len, feature_dim = queries_ref.shape[1:]
    length = held.shape[2]

    def fetch(group, u):
        half = lax.rem(group, 2)
        return pltpu.make_async_copy(
            passages_ref.at[row_ref[group * GROUP + u]], held.at[half, u], arrived.at[half, u]
        )

    for u in range(GROUP):
        fetch(0, u).start()

    @pl.loop(0, groups)
    def _(group):
        first = group * GROUP

        @pl.when(group + 1 < groups)
        def _():
            for u in range(GROUP):
                fetch(group + 1, u).start()

        for u in range(GROUP):
            fetch(group, u).wait()
        half = lax.rem(group, 2)
        pairs, scores = [], []
        for u in range(0, GROUP, 2):
            tile = held[half, u : u + 2].reshape(2 * length, feature_dim)
            stacked = jnp.concatenate(
                [queries_ref[qid_ref[first + u]], queries_ref[qid_ref[first + u + 1]]], axis=0
            )
            both = lax.dot_general(
                stacked, tile, (((1,), (1,)), ((), ())), preferred_element_type=jnp.float32
            )
            pairs.append(tile)
            scores += [both[:query_len, :length], both[query_len:, length:]]
        largest = [jnp.max(s, axis=1, keepdims=True) for s in scores]
        raised = [jnp.exp(s - m) for s, m in zip(scores, largest)]
        totals = [jnp.sum(r, axis=1, keepdims=True) for r in raised]
        guesses = [pl.reciprocal(t, approx=True) for t in totals]
        inverse = [g * (2.0 - t * g) for g, t in zip(guesses, totals)]
        weights = [(r * v).astype(jnp.bfloat16) for r, v in zip(raised, inverse)]
        blank = jnp.zeros((query_len, length), jnp.bfloat16)
        for u in range(0, GROUP, 2):
            spread = jnp.concatenate(
                [
                    jnp.concatenate([weights[u], blank], axis=1),
                    jnp.concatenate([blank, weights[u + 1]], axis=1),
                ],
                axis=0,
            )
            both = jnp.dot(spread, pairs[u // 2], preferred_element_type=jnp.float32)
            basis_ref[first + u] = both[:query_len].astype(jnp.bfloat16)
            basis_ref[first + u + 1] = both[query_len:].astype(jnp.bfloat16)
        rows = [
            jnp.sum(quarter_sum(m) + jnp.log(quarter_product(t)), axis=0, keepdims=True)
            for m, t in zip(largest, totals)
        ]
        sim_ref[pl.ds(pl.multiple_of(first, GROUP), GROUP), :] = jnp.broadcast_to(
            jnp.concatenate(rows, axis=0), (GROUP, sim_ref.shape[1])
        )


def pair_terms(rows, qids, queries, passages):
    slots = rows.shape[0]
    query_len, feature_dim = queries.shape[1:]
    return pl.pallas_call(
        pair_kernel,
        out_shape=(
            jax.ShapeDtypeStruct((slots, query_len, feature_dim), jnp.bfloat16),
            jax.ShapeDtypeStruct((slots, 128), jnp.float32),
        ),
        in_specs=[pl.BlockSpec(memory_space=pltpu.SMEM)] * 2
        + [pl.BlockSpec(memory_space=pltpu.VMEM), pl.BlockSpec(memory_space=pltpu.HBM)],
        out_specs=(pl.BlockSpec(memory_space=pltpu.VMEM),) * 2,
        scratch_shapes=[
            pltpu.VMEM((2, GROUP) + passages.shape[1:], passages.dtype),
            pltpu.SemaphoreType.DMA((2, GROUP)),
        ],
        compiler_params=pltpu.CompilerParams(vmem_limit_bytes=48 * 1024 * 1024),
    )(rows, qids, queries, passages)


def greet(shards, me):
    barrier = pltpu.get_barrier_semaphore()
    for step in range(1, shards):
        pl.semaphore_signal(
            barrier, inc=1, device_id={"bank": lax.rem(me + step, shards)}, device_id_type=MESH
        )
    pl.semaphore_wait(barrier, shards - 1)


def gather_kernel(shards, inner, q_ref, info_ref, all_q_ref, all_info_ref, sends, recvs, isends, irecvs):
    outer = shards // inner
    me = lax.axis_index("bank")
    z, y = me // inner, lax.rem(me, inner)
    rows = q_ref.shape[0]

    def place(index):
        return pl.ds(pl.multiple_of(index * rows, rows), rows)

    def peer(dz, dy):
        return lax.rem(z + dz, outer) * inner + lax.rem(y + dy, inner)

    def send(src, block, slot, target):
        copy = pltpu.make_async_remote_copy(
            src_ref=src,
            dst_ref=all_q_ref.at[place(block)],
            send_sem=sends.at[slot],
            recv_sem=recvs.at[slot],
            device_id={"bank": target},
            device_id_type=MESH,
        )
        copy.start()
        return copy

    greet(shards, me)
    copies = {}
    for dz in range(1, outer):
        copies[dz * inner] = send(q_ref, me, dz * inner, peer(dz, 0))
    small = []
    for step in range(1, shards):
        copy = pltpu.make_async_remote_copy(
            src_ref=info_ref,
            dst_ref=all_info_ref.at[place(me)],
            send_sem=isends.at[step],
            recv_sem=irecvs.at[step],
            device_id={"bank": lax.rem(me + step, shards)},
            device_id_type=MESH,
        )
        copy.start()
        small.append(copy)
    for dy in range(1, inner):
        copies[dy] = send(q_ref, me, dy, peer(0, dy))
    all_q_ref[place(me)] = q_ref[...]
    all_info_ref[place(me)] = info_ref[...]
    for dz in range(1, outer):
        copies[dz * inner].wait_recv()
        source = lax.rem(z + outer - dz, outer) * inner + y
        for dy in range(1, inner):
            copies[dz * inner + dy] = send(
                all_q_ref.at[place(source)], source, dz * inner + dy, peer(0, dy)
            )
    for slot, copy in copies.items():
        if slot < inner or slot % inner:
            copy.wait_recv()
        copy.wait_send()
    for copy in small:
        copy.wait()


def gather_queries(queries, info):
    shards = lax.axis_size("bank")
    inner = 1
    while (2 * inner) ** 2 <= shards:
        inner *= 2
    vmem = pl.BlockSpec(memory_space=pltpu.VMEM)
    return pl.pallas_call(
        functools.partial(gather_kernel, shards, inner),
        out_shape=(
            jax.ShapeDtypeStruct((shards * queries.shape[0],) + queries.shape[1:], queries.dtype),
            jax.ShapeDtypeStruct((shards * info.shape[0], info.shape[1]), info.dtype),
        ),
        in_specs=[vmem, vmem],
        out_specs=(vmem, vmem),
        scratch_shapes=[pltpu.SemaphoreType.DMA((shards,))] * 4,
        compiler_params=pltpu.CompilerParams(
            collective_id=0, has_side_effects=True, vmem_limit_bytes=16 * 1024 * 1024
        ),
    )(queries, info)


def contrast_kernel(shards, sim_ref, meta_ref, coef_ref, loss_ref, slots, sends, recvs):
    me = lax.axis_index("bank")
    width = coef_ref.shape[1]
    capacity = sim_ref.shape[0]
    meta = meta_ref[...]
    lane = lax.broadcasted_iota(jnp.int32, (capacity, width), 1)
    chosen = meta == lane * 2 + 1
    match = chosen | (meta == lane * 2)
    table = jnp.where(match, sim_ref[:, :1], -jnp.inf)
    largest = jnp.max(table, axis=0, keepdims=True)
    safe = jnp.where(largest == -jnp.inf, 0.0, largest)
    partial = jnp.sum(jnp.exp(table - safe), axis=0, keepdims=True)
    wanted = jnp.sum(jnp.where(chosen, table, 0.0), axis=0, keepdims=True)
    slots[me] = jnp.concatenate([largest, partial, wanted, jnp.zeros((5, width), jnp.float32)], axis=0)
    greet(shards, me)
    copies = []
    for step in range(1, shards):
        copy = pltpu.make_async_remote_copy(
            src_ref=slots.at[me],
            dst_ref=slots.at[me],
            send_sem=sends.at[step],
            recv_sem=recvs.at[step],
            device_id={"bank": lax.rem(me + step, shards)},
            device_id_type=MESH,
        )
        copy.start()
        copies.append(copy)
    for copy in copies:
        copy.wait()
    tops = [slots[b, 0:1, :] for b in range(shards)]
    top = functools.reduce(jnp.maximum, tops)
    top = jnp.where(top == -jnp.inf, 0.0, top)
    total = sum(slots[b, 1:2, :] * jnp.exp(tops[b] - top) for b in range(shards))
    picked = sum(slots[b, 2:3, :] for b in range(shards))
    loss_ref[...] = jnp.broadcast_to(top + jnp.log(total) - picked, loss_ref.shape)
    total = jnp.where(total == 0.0, 1.0, total)
    shares = jnp.exp(table - top) / total
    coef_ref[...] = (shares - jnp.where(chosen, 1.0, 0.0)).astype(coef_ref.dtype)


def contrast(sims, meta, group):
    shards = lax.axis_size("bank")
    width = -(-group // 128) * 128
    vmem = pl.BlockSpec(memory_space=pltpu.VMEM)
    return pl.pallas_call(
        functools.partial(contrast_kernel, shards),
        out_shape=(
            jax.ShapeDtypeStruct((sims.shape[0], width), jnp.bfloat16),
            jax.ShapeDtypeStruct((8, width), jnp.float32),
        ),
        in_specs=[vmem, vmem],
        out_specs=(vmem, vmem),
        scratch_shapes=[
            pltpu.VMEM((shards, 8, width), jnp.float32),
            pltpu.SemaphoreType.DMA((shards,)),
            pltpu.SemaphoreType.DMA((shards,)),
        ],
        compiler_params=pltpu.CompilerParams(
            collective_id=1, has_side_effects=True, vmem_limit_bytes=16 * 1024 * 1024
        ),
    )(sims, meta)


def slot_list(storage, positive, holdings, capacity):
    count, listed = storage.shape
    me = lax.axis_index("bank")
    owned = (storage // holdings == me).reshape(-1)
    entry = jnp.arange(count * listed, dtype=jnp.int32)
    picked = (jnp.arange(listed, dtype=jnp.int32)[None, :] == positive[:, None]).astype(jnp.int32)
    query = entry // listed
    code = (query * 2 + picked.reshape(-1)) * holdings + (storage % holdings).reshape(-1)
    position = jnp.cumsum(owned.astype(jnp.int32)) - 1
    target = jnp.where(owned, position, -1)
    here = target[None, :] == jnp.arange(capacity, dtype=jnp.int32)[:, None]
    table = jnp.sum(jnp.where(here, code[None, :] + 1, 0), axis=1) - 1
    meta = jnp.where(table >= 0, table // holdings, -1)
    table = jnp.maximum(table, 0)
    return table % holdings, table // holdings // 2, meta


def body(queries, passages, passage_home, candidates, positive):
    shards = lax.axis_size("bank")
    query_rows, query_len, feature_dim = queries.shape
    listed = candidates.shape[1]
    holdings = passages.shape[0]
    capacity = 3 * query_rows * listed
    group = shards * query_rows
    info = jnp.concatenate([passage_home[candidates], positive[:, None]], axis=1)
    info = jnp.pad(info, ((0, 0), (0, 128 - info.shape[1])))
    all_queries, infos = gather_queries(queries, info)
    rows, qids, meta = slot_list(infos[:, :listed], infos[:, listed], holdings, capacity)
    basis, sims = pair_terms(rows, qids, all_queries, passages)
    coefficients, losses = contrast(sims, meta[:, None], group)
    mine = lax.axis_index("bank") * query_rows
    losses = lax.dynamic_slice_in_dim(losses[0], mine, query_rows, 0)
    part = lax.dot_general(
        coefficients[:, :group],
        basis.reshape(capacity, query_len * feature_dim),
        (((0,), (0,)), ((), ())),
        preferred_element_type=jnp.float32,
    ).astype(jnp.bfloat16)
    parts = lax.all_to_all(
        part.reshape(shards, query_rows, query_len * feature_dim), "bank", 0, 0, tiled=True
    )
    gradient = jnp.sum(parts.astype(jnp.float32), axis=0)
    return (losses, gradient.reshape(query_rows, query_len, feature_dim))


def solution(mesh):
    return jax.shard_map(
        body,
        mesh=mesh,
        in_specs=(
            P(("query", "bank"), None, None),
            P("bank", None, None),
            P(),
            P(("query", "bank"), None),
            P(("query", "bank")),
        ),
        out_specs=(P(("query", "bank")), P(("query", "bank"), None, None)),
        check_vma=False,
    )
```

```python
import functools

import jax
import jax.numpy as jnp
from jax import lax
from jax.experimental import pallas as pl
from jax.experimental.pallas import tpu as pltpu
from jax.sharding import PartitionSpec as P

GROUP = 48


MESH = pl.DeviceIdType.MESH


def quarter_sum(x):
    n = x.shape[0] // 4
    return (x[:n] + x[n : 2 * n]) + (x[2 * n : 3 * n] + x[3 * n :])


def quarter_product(x):
    n = x.shape[0] // 4
    return (x[:n] * x[n : 2 * n]) * (x[2 * n : 3 * n] * x[3 * n :])


def pair_kernel(row_ref, qid_ref, queries_ref, passages_ref, basis_ref, sim_ref, held, arrived):
    groups = row_ref.shape[0] // GROUP
    query_len, feature_dim = queries_ref.shape[1:]
    length = held.shape[2]

    def fetch(group, u):
        half = lax.rem(group, 2)
        return pltpu.make_async_copy(
            passages_ref.at[row_ref[group * GROUP + u]], held.at[half, u], arrived.at[half, u]
        )

    for u in range(GROUP):
        fetch(0, u).start()

    @pl.loop(0, groups)
    def _(group):
        first = group * GROUP

        @pl.when(group + 1 < groups)
        def _():
            for u in range(GROUP):
                fetch(group + 1, u).start()

        for u in range(GROUP):
            fetch(group, u).wait()
        half = lax.rem(group, 2)
        pairs, scores = [], []
        for u in range(0, GROUP, 2):
            tile = held[half, u : u + 2].reshape(2 * length, feature_dim)
            stacked = jnp.concatenate(
                [queries_ref[qid_ref[first + u]], queries_ref[qid_ref[first + u + 1]]], axis=0
            )
            both = lax.dot_general(
                stacked, tile, (((1,), (1,)), ((), ())), preferred_element_type=jnp.float32
            )
            pairs.append(tile)
            scores += [both[:query_len, :length], both[query_len:, length:]]
        largest = [jnp.max(s, axis=1, keepdims=True) for s in scores]
        raised = [jnp.exp(s - m) for s, m in zip(scores, largest)]
        totals = [jnp.sum(r, axis=1, keepdims=True) for r in raised]
        guesses = [pl.reciprocal(t, approx=True) for t in totals]
        inverse = [g * (2.0 - t * g) for g, t in zip(guesses, totals)]
        weights = [(r * v).astype(jnp.bfloat16) for r, v in zip(raised, inverse)]
        blank = jnp.zeros((query_len, length), jnp.bfloat16)
        for u in range(0, GROUP, 2):
            spread = jnp.concatenate(
                [
                    jnp.concatenate([weights[u], blank], axis=1),
                    jnp.concatenate([blank, weights[u + 1]], axis=1),
                ],
                axis=0,
            )
            both = jnp.dot(spread, pairs[u // 2], preferred_element_type=jnp.float32)
            basis_ref[first + u] = both[:query_len].astype(jnp.bfloat16)
            basis_ref[first + u + 1] = both[query_len:].astype(jnp.bfloat16)
        rows = [
            jnp.sum(quarter_sum(m) + jnp.log(quarter_product(t)), axis=0, keepdims=True)
            for m, t in zip(largest, totals)
        ]
        sim_ref[pl.ds(pl.multiple_of(first, GROUP), GROUP), :] = jnp.broadcast_to(
            jnp.concatenate(rows, axis=0), (GROUP, sim_ref.shape[1])
        )


def pair_terms(rows, qids, queries, passages):
    slots = rows.shape[0]
    query_len, feature_dim = queries.shape[1:]
    return pl.pallas_call(
        pair_kernel,
        out_shape=(
            jax.ShapeDtypeStruct((slots, query_len, feature_dim), jnp.bfloat16),
            jax.ShapeDtypeStruct((slots, 128), jnp.float32),
        ),
        in_specs=[pl.BlockSpec(memory_space=pltpu.SMEM)] * 2
        + [pl.BlockSpec(memory_space=pltpu.VMEM), pl.BlockSpec(memory_space=pltpu.HBM)],
        out_specs=(pl.BlockSpec(memory_space=pltpu.VMEM),) * 2,
        scratch_shapes=[
            pltpu.VMEM((2, GROUP) + passages.shape[1:], passages.dtype),
            pltpu.SemaphoreType.DMA((2, GROUP)),
        ],
        compiler_params=pltpu.CompilerParams(vmem_limit_bytes=48 * 1024 * 1024),
    )(rows, qids, queries, passages)


def greet(shards, me):
    barrier = pltpu.get_barrier_semaphore()
    for step in range(1, shards):
        pl.semaphore_signal(
            barrier, inc=1, device_id={"bank": lax.rem(me + step, shards)}, device_id_type=MESH
        )
    pl.semaphore_wait(barrier, shards - 1)


def gather_kernel(shards, inner, q_ref, info_ref, all_q_ref, all_info_ref, sends, recvs, isends, irecvs):
    outer = shards // inner
    me = lax.axis_index("bank")
    z, y = me // inner, lax.rem(me, inner)
    rows = q_ref.shape[0]

    def place(index):
        return pl.ds(pl.multiple_of(index * rows, rows), rows)

    def peer(dz, dy):
        return lax.rem(z + dz, outer) * inner + lax.rem(y + dy, inner)

    def send(src, block, slot, target):
        copy = pltpu.make_async_remote_copy(
            src_ref=src,
            dst_ref=all_q_ref.at[place(block)],
            send_sem=sends.at[slot],
            recv_sem=recvs.at[slot],
            device_id={"bank": target},
            device_id_type=MESH,
        )
        copy.start()
        return copy

    greet(shards, me)
    copies = {}
    for dz in range(1, outer):
        copies[dz * inner] = send(q_ref, me, dz * inner, peer(dz, 0))
    small = []
    for step in range(1, shards):
        copy = pltpu.make_async_remote_copy(
            src_ref=info_ref,
            dst_ref=all_info_ref.at[place(me)],
            send_sem=isends.at[step],
            recv_sem=irecvs.at[step],
            device_id={"bank": lax.rem(me + step, shards)},
            device_id_type=MESH,
        )
        copy.start()
        small.append(copy)
    for dy in range(1, inner):
        copies[dy] = send(q_ref, me, dy, peer(0, dy))
    all_q_ref[place(me)] = q_ref[...]
    all_info_ref[place(me)] = info_ref[...]
    for dz in range(1, outer):
        copies[dz * inner].wait_recv()
        source = lax.rem(z + outer - dz, outer) * inner + y
        for dy in range(1, inner):
            copies[dz * inner + dy] = send(
                all_q_ref.at[place(source)], source, dz * inner + dy, peer(0, dy)
            )
    for slot, copy in copies.items():
        if slot < inner or slot % inner:
            copy.wait_recv()
        copy.wait_send()
    for copy in small:
        copy.wait()


def gather_queries(queries, info):
    shards = lax.axis_size("bank")
    inner = 1
    while (2 * inner) ** 2 <= shards:
        inner *= 2
    vmem = pl.BlockSpec(memory_space=pltpu.VMEM)
    return pl.pallas_call(
        functools.partial(gather_kernel, shards, inner),
        out_shape=(
            jax.ShapeDtypeStruct((shards * queries.shape[0],) + queries.shape[1:], queries.dtype),
            jax.ShapeDtypeStruct((shards * info.shape[0], info.shape[1]), info.dtype),
        ),
        in_specs=[vmem, vmem],
        out_specs=(vmem, vmem),
        scratch_shapes=[pltpu.SemaphoreType.DMA((shards,))] * 4,
        compiler_params=pltpu.CompilerParams(
            collective_id=0, has_side_effects=True, vmem_limit_bytes=16 * 1024 * 1024
        ),
    )(queries, info)


def contrast_kernel(shards, sim_ref, meta_ref, coef_ref, loss_ref, slots, sends, recvs):
    me = lax.axis_index("bank")
    width = coef_ref.shape[1]
    capacity = sim_ref.shape[0]
    meta = meta_ref[...]
    lane = lax.broadcasted_iota(jnp.int32, (capacity, width), 1)
    chosen = meta == lane * 2 + 1
    match = chosen | (meta == lane * 2)
    table = jnp.where(match, sim_ref[:, :1], -jnp.inf)
    largest = jnp.max(table, axis=0, keepdims=True)
    safe = jnp.where(largest == -jnp.inf, 0.0, largest)
    partial = jnp.sum(jnp.exp(table - safe), axis=0, keepdims=True)
    wanted = jnp.sum(jnp.where(chosen, table, 0.0), axis=0, keepdims=True)
    slots[me] = jnp.concatenate([largest, partial, wanted, jnp.zeros((5, width), jnp.float32)], axis=0)
    greet(shards, me)
    copies = []
    for step in range(1, shards):
        copy = pltpu.make_async_remote_copy(
            src_ref=slots.at[me],
            dst_ref=slots.at[me],
            send_sem=sends.at[step],
            recv_sem=recvs.at[step],
            device_id={"bank": lax.rem(me + step, shards)},
            device_id_type=MESH,
        )
        copy.start()
        copies.append(copy)
    for copy in copies:
        copy.wait()
    tops = [slots[b, 0:1, :] for b in range(shards)]
    top = functools.reduce(jnp.maximum, tops)
    top = jnp.where(top == -jnp.inf, 0.0, top)
    total = sum(slots[b, 1:2, :] * jnp.exp(tops[b] - top) for b in range(shards))
    picked = sum(slots[b, 2:3, :] for b in range(shards))
    loss_ref[...] = jnp.broadcast_to(top + jnp.log(total) - picked, loss_ref.shape)
    total = jnp.where(total == 0.0, 1.0, total)
    shares = jnp.exp(table - top) / total
    coef_ref[...] = (shares - jnp.where(chosen, 1.0, 0.0)).astype(coef_ref.dtype)


def contrast(sims, meta, group):
    shards = lax.axis_size("bank")
    width = -(-group // 128) * 128
    vmem = pl.BlockSpec(memory_space=pltpu.VMEM)
    return pl.pallas_call(
        functools.partial(contrast_kernel, shards),
        out_shape=(
            jax.ShapeDtypeStruct((sims.shape[0], width), jnp.bfloat16),
            jax.ShapeDtypeStruct((8, width), jnp.float32),
        ),
        in_specs=[vmem, vmem],
        out_specs=(vmem, vmem),
        scratch_shapes=[
            pltpu.VMEM((shards, 8, width), jnp.float32),
            pltpu.SemaphoreType.DMA((shards,)),
            pltpu.SemaphoreType.DMA((shards,)),
        ],
        compiler_params=pltpu.CompilerParams(
            collective_id=1, has_side_effects=True, vmem_limit_bytes=16 * 1024 * 1024
        ),
    )(sims, meta)


def slot_list(storage, positive, holdings, capacity):
    count, listed = storage.shape
    me = lax.axis_index("bank")
    owned = (storage // holdings == me).reshape(-1)
    entry = jnp.arange(count * listed, dtype=jnp.int32)
    picked = (jnp.arange(listed, dtype=jnp.int32)[None, :] == positive[:, None]).astype(jnp.int32)
    query = entry // listed
    code = (query * 2 + picked.reshape(-1)) * holdings + (storage % holdings).reshape(-1)
    position = jnp.cumsum(owned.astype(jnp.int32)) - 1
    target = jnp.where(owned, position, -1)
    here = target[None, :] == jnp.arange(capacity, dtype=jnp.int32)[:, None]
    table = jnp.sum(jnp.where(here, code[None, :] + 1, 0), axis=1) - 1
    meta = jnp.where(table >= 0, table // holdings, -1)
    table = jnp.maximum(table, 0)
    return table % holdings, table // holdings // 2, meta


def body(queries, passages, passage_home, candidates, positive):
    shards = lax.axis_size("bank")
    query_rows, query_len, feature_dim = queries.shape
    listed = candidates.shape[1]
    holdings = passages.shape[0]
    capacity = 3 * query_rows * listed
    group = shards * query_rows
    info = jnp.concatenate([passage_home[candidates], positive[:, None]], axis=1)
    info = jnp.pad(info, ((0, 0), (0, 128 - info.shape[1])))
    all_queries, infos = gather_queries(queries, info)
    rows, qids, meta = slot_list(infos[:, :listed], infos[:, listed], holdings, capacity)
    basis, sims = pair_terms(rows, qids, all_queries, passages)
    coefficients, losses = contrast(sims, meta[:, None], group)
    mine = lax.axis_index("bank") * query_rows
    losses = lax.dynamic_slice_in_dim(losses[0], mine, query_rows, 0)
    part = lax.dot_general(
        coefficients[:, :group],
        basis.reshape(capacity, query_len * feature_dim),
        (((0,), (0,)), ((), ())),
        preferred_element_type=jnp.float32,
    ).astype(jnp.bfloat16)
    parts = lax.all_to_all(
        part.reshape(shards, query_rows, query_len * feature_dim), "bank", 0, 0, tiled=True
    )
    gradient = jnp.sum(parts.astype(jnp.float32), axis=0)
    return (losses, gradient.reshape(query_rows, query_len, feature_dim))


def solution(mesh):
    return jax.shard_map(
        body,
        mesh=mesh,
        in_specs=(
            P(("query", "bank"), None, None),
            P("bank", None, None),
            P(),
            P(("query", "bank"), None),
            P(("query", "bank")),
        ),
        out_specs=(P(("query", "bank")), P(("query", "bank"), None, None)),
        check_vma=False,
    )
```

```python
import functools

import jax
import jax.numpy as jnp
from jax import lax
from jax.experimental import pallas as pl
from jax.experimental.pallas import tpu as pltpu
from jax.sharding import PartitionSpec as P

GROUP = 64


MESH = pl.DeviceIdType.MESH


def quarter_sum(x):
    n = x.shape[0] // 4
    return (x[:n] + x[n : 2 * n]) + (x[2 * n : 3 * n] + x[3 * n :])


def quarter_product(x):
    n = x.shape[0] // 4
    return (x[:n] * x[n : 2 * n]) * (x[2 * n : 3 * n] * x[3 * n :])


def pair_kernel(row_ref, qid_ref, queries_ref, passages_ref, basis_ref, sim_ref, held, arrived):
    groups = row_ref.shape[0] // GROUP
    query_len, feature_dim = queries_ref.shape[1:]
    length = held.shape[2]

    def fetch(group, u):
        half = lax.rem(group, 2)
        return pltpu.make_async_copy(
            passages_ref.at[row_ref[group * GROUP + u]], held.at[half, u], arrived.at[half, u]
        )

    for u in range(GROUP):
        fetch(0, u).start()

    @pl.loop(0, groups)
    def _(group):
        first = group * GROUP

        @pl.when(group + 1 < groups)
        def _():
            for u in range(GROUP):
                fetch(group + 1, u).start()

        for u in range(GROUP):
            fetch(group, u).wait()
        half = lax.rem(group, 2)
        pairs, scores = [], []
        for u in range(0, GROUP, 2):
            tile = held[half, u : u + 2].reshape(2 * length, feature_dim)
            stacked = jnp.concatenate(
                [queries_ref[qid_ref[first + u]], queries_ref[qid_ref[first + u + 1]]], axis=0
            )
            both = lax.dot_general(
                stacked, tile, (((1,), (1,)), ((), ())), preferred_element_type=jnp.float32
            )
            pairs.append(tile)
            scores += [both[:query_len, :length], both[query_len:, length:]]
        largest = [jnp.max(s, axis=1, keepdims=True) for s in scores]
        raised = [jnp.exp(s - m) for s, m in zip(scores, largest)]
        totals = [jnp.sum(r, axis=1, keepdims=True) for r in raised]
        guesses = [pl.reciprocal(t, approx=True) for t in totals]
        inverse = [g * (2.0 - t * g) for g, t in zip(guesses, totals)]
        weights = [(r * v).astype(jnp.bfloat16) for r, v in zip(raised, inverse)]
        blank = jnp.zeros((query_len, length), jnp.bfloat16)
        for u in range(0, GROUP, 2):
            spread = jnp.concatenate(
                [
                    jnp.concatenate([weights[u], blank], axis=1),
                    jnp.concatenate([blank, weights[u + 1]], axis=1),
                ],
                axis=0,
            )
            both = jnp.dot(spread, pairs[u // 2], preferred_element_type=jnp.float32)
            basis_ref[first + u] = both[:query_len].astype(jnp.bfloat16)
            basis_ref[first + u + 1] = both[query_len:].astype(jnp.bfloat16)
        rows = [
            jnp.sum(quarter_sum(m) + jnp.log(quarter_product(t)), axis=0, keepdims=True)
            for m, t in zip(largest, totals)
        ]
        sim_ref[pl.ds(pl.multiple_of(first, GROUP), GROUP), :] = jnp.broadcast_to(
            jnp.concatenate(rows, axis=0), (GROUP, sim_ref.shape[1])
        )


def pair_terms(rows, qids, queries, passages):
    slots = rows.shape[0]
    query_len, feature_dim = queries.shape[1:]
    return pl.pallas_call(
        pair_kernel,
        out_shape=(
            jax.ShapeDtypeStruct((slots, query_len, feature_dim), jnp.bfloat16),
            jax.ShapeDtypeStruct((slots, 128), jnp.float32),
        ),
        in_specs=[pl.BlockSpec(memory_space=pltpu.SMEM)] * 2
        + [pl.BlockSpec(memory_space=pltpu.VMEM), pl.BlockSpec(memory_space=pltpu.HBM)],
        out_specs=(pl.BlockSpec(memory_space=pltpu.VMEM),) * 2,
        scratch_shapes=[
            pltpu.VMEM((2, GROUP) + passages.shape[1:], passages.dtype),
            pltpu.SemaphoreType.DMA((2, GROUP)),
        ],
        compiler_params=pltpu.CompilerParams(vmem_limit_bytes=48 * 1024 * 1024),
    )(rows, qids, queries, passages)


def greet(shards, me):
    barrier = pltpu.get_barrier_semaphore()
    for step in range(1, shards):
        pl.semaphore_signal(
            barrier, inc=1, device_id={"bank": lax.rem(me + step, shards)}, device_id_type=MESH
        )
    pl.semaphore_wait(barrier, shards - 1)


def gather_kernel(shards, inner, q_ref, info_ref, all_q_ref, all_info_ref, sends, recvs, isends, irecvs):
    outer = shards // inner
    me = lax.axis_index("bank")
    z, y = me // inner, lax.rem(me, inner)
    rows = q_ref.shape[0]

    def place(index):
        return pl.ds(pl.multiple_of(index * rows, rows), rows)

    def peer(dz, dy):
        return lax.rem(z + dz, outer) * inner + lax.rem(y + dy, inner)

    def send(src, block, slot, target):
        copy = pltpu.make_async_remote_copy(
            src_ref=src,
            dst_ref=all_q_ref.at[place(block)],
            send_sem=sends.at[slot],
            recv_sem=recvs.at[slot],
            device_id={"bank": target},
            device_id_type=MESH,
        )
        copy.start()
        return copy

    greet(shards, me)
    copies = {}
    for dz in range(1, outer):
        copies[dz * inner] = send(q_ref, me, dz * inner, peer(dz, 0))
    small = []
    for step in range(1, shards):
        copy = pltpu.make_async_remote_copy(
            src_ref=info_ref,
            dst_ref=all_info_ref.at[place(me)],
            send_sem=isends.at[step],
            recv_sem=irecvs.at[step],
            device_id={"bank": lax.rem(me + step, shards)},
            device_id_type=MESH,
        )
        copy.start()
        small.append(copy)
    for dy in range(1, inner):
        copies[dy] = send(q_ref, me, dy, peer(0, dy))
    all_q_ref[place(me)] = q_ref[...]
    all_info_ref[place(me)] = info_ref[...]
    for dz in range(1, outer):
        copies[dz * inner].wait_recv()
        source = lax.rem(z + outer - dz, outer) * inner + y
        for dy in range(1, inner):
            copies[dz * inner + dy] = send(
                all_q_ref.at[place(source)], source, dz * inner + dy, peer(0, dy)
            )
    for slot, copy in copies.items():
        if slot < inner or slot % inner:
            copy.wait_recv()
        copy.wait_send()
    for copy in small:
        copy.wait()


def gather_queries(queries, info):
    shards = lax.axis_size("bank")
    inner = 1
    while (2 * inner) ** 2 <= shards:
        inner *= 2
    vmem = pl.BlockSpec(memory_space=pltpu.VMEM)
    return pl.pallas_call(
        functools.partial(gather_kernel, shards, inner),
        out_shape=(
            jax.ShapeDtypeStruct((shards * queries.shape[0],) + queries.shape[1:], queries.dtype),
            jax.ShapeDtypeStruct((shards * info.shape[0], info.shape[1]), info.dtype),
        ),
        in_specs=[vmem, vmem],
        out_specs=(vmem, vmem),
        scratch_shapes=[pltpu.SemaphoreType.DMA((shards,))] * 4,
        compiler_params=pltpu.CompilerParams(
            collective_id=0, has_side_effects=True, vmem_limit_bytes=16 * 1024 * 1024
        ),
    )(queries, info)


def contrast_kernel(shards, sim_ref, meta_ref, coef_ref, loss_ref, slots, sends, recvs):
    me = lax.axis_index("bank")
    width = coef_ref.shape[1]
    capacity = sim_ref.shape[0]
    meta = meta_ref[...]
    lane = lax.broadcasted_iota(jnp.int32, (capacity, width), 1)
    chosen = meta == lane * 2 + 1
    match = chosen | (meta == lane * 2)
    table = jnp.where(match, sim_ref[:, :1], -jnp.inf)
    largest = jnp.max(table, axis=0, keepdims=True)
    safe = jnp.where(largest == -jnp.inf, 0.0, largest)
    partial = jnp.sum(jnp.exp(table - safe), axis=0, keepdims=True)
    wanted = jnp.sum(jnp.where(chosen, table, 0.0), axis=0, keepdims=True)
    slots[me] = jnp.concatenate([largest, partial, wanted, jnp.zeros((5, width), jnp.float32)], axis=0)
    greet(shards, me)
    copies = []
    for step in range(1, shards):
        copy = pltpu.make_async_remote_copy(
            src_ref=slots.at[me],
            dst_ref=slots.at[me],
            send_sem=sends.at[step],
            recv_sem=recvs.at[step],
            device_id={"bank": lax.rem(me + step, shards)},
            device_id_type=MESH,
        )
        copy.start()
        copies.append(copy)
    for copy in copies:
        copy.wait()
    tops = [slots[b, 0:1, :] for b in range(shards)]
    top = functools.reduce(jnp.maximum, tops)
    top = jnp.where(top == -jnp.inf, 0.0, top)
    total = sum(slots[b, 1:2, :] * jnp.exp(tops[b] - top) for b in range(shards))
    picked = sum(slots[b, 2:3, :] for b in range(shards))
    loss_ref[...] = jnp.broadcast_to(top + jnp.log(total) - picked, loss_ref.shape)
    total = jnp.where(total == 0.0, 1.0, total)
    shares = jnp.exp(table - top) / total
    coef_ref[...] = (shares - jnp.where(chosen, 1.0, 0.0)).astype(coef_ref.dtype)


def contrast(sims, meta, group):
    shards = lax.axis_size("bank")
    width = -(-group // 128) * 128
    vmem = pl.BlockSpec(memory_space=pltpu.VMEM)
    return pl.pallas_call(
        functools.partial(contrast_kernel, shards),
        out_shape=(
            jax.ShapeDtypeStruct((sims.shape[0], width), jnp.bfloat16),
            jax.ShapeDtypeStruct((8, width), jnp.float32),
        ),
        in_specs=[vmem, vmem],
        out_specs=(vmem, vmem),
        scratch_shapes=[
            pltpu.VMEM((shards, 8, width), jnp.float32),
            pltpu.SemaphoreType.DMA((shards,)),
            pltpu.SemaphoreType.DMA((shards,)),
        ],
        compiler_params=pltpu.CompilerParams(
            collective_id=1, has_side_effects=True, vmem_limit_bytes=16 * 1024 * 1024
        ),
    )(sims, meta)


def slot_list(storage, positive, holdings, capacity):
    count, listed = storage.shape
    me = lax.axis_index("bank")
    owned = (storage // holdings == me).reshape(-1)
    entry = jnp.arange(count * listed, dtype=jnp.int32)
    picked = (jnp.arange(listed, dtype=jnp.int32)[None, :] == positive[:, None]).astype(jnp.int32)
    query = entry // listed
    code = (query * 2 + picked.reshape(-1)) * holdings + (storage % holdings).reshape(-1)
    position = jnp.cumsum(owned.astype(jnp.int32)) - 1
    target = jnp.where(owned, position, -1)
    here = target[None, :] == jnp.arange(capacity, dtype=jnp.int32)[:, None]
    table = jnp.sum(jnp.where(here, code[None, :] + 1, 0), axis=1) - 1
    meta = jnp.where(table >= 0, table // holdings, -1)
    table = jnp.maximum(table, 0)
    return table % holdings, table // holdings // 2, meta


def body(queries, passages, passage_home, candidates, positive):
    shards = lax.axis_size("bank")
    query_rows, query_len, feature_dim = queries.shape
    listed = candidates.shape[1]
    holdings = passages.shape[0]
    capacity = 3 * query_rows * listed
    group = shards * query_rows
    info = jnp.concatenate([passage_home[candidates], positive[:, None]], axis=1)
    info = jnp.pad(info, ((0, 0), (0, 128 - info.shape[1])))
    all_queries, infos = gather_queries(queries, info)
    rows, qids, meta = slot_list(infos[:, :listed], infos[:, listed], holdings, capacity)
    basis, sims = pair_terms(rows, qids, all_queries, passages)
    coefficients, losses = contrast(sims, meta[:, None], group)
    mine = lax.axis_index("bank") * query_rows
    losses = lax.dynamic_slice_in_dim(losses[0], mine, query_rows, 0)
    part = lax.dot_general(
        coefficients[:, :group],
        basis.reshape(capacity, query_len * feature_dim),
        (((0,), (0,)), ((), ())),
        preferred_element_type=jnp.float32,
    ).astype(jnp.bfloat16)
    parts = lax.all_to_all(
        part.reshape(shards, query_rows, query_len * feature_dim), "bank", 0, 0, tiled=True
    )
    gradient = jnp.sum(parts.astype(jnp.float32), axis=0)
    return (losses, gradient.reshape(query_rows, query_len, feature_dim))


def solution(mesh):
    return jax.shard_map(
        body,
        mesh=mesh,
        in_specs=(
            P(("query", "bank"), None, None),
            P("bank", None, None),
            P(),
            P(("query", "bank"), None),
            P(("query", "bank")),
        ),
        out_specs=(P(("query", "bank")), P(("query", "bank"), None, None)),
        check_vma=False,
    )
```

```python
import functools

import jax
import jax.numpy as jnp
from jax import lax
from jax.experimental import pallas as pl
from jax.experimental.pallas import tpu as pltpu
from jax.sharding import PartitionSpec as P

GROUP = 96


MESH = pl.DeviceIdType.MESH


def quarter_sum(x):
    n = x.shape[0] // 4
    return (x[:n] + x[n : 2 * n]) + (x[2 * n : 3 * n] + x[3 * n :])


def quarter_product(x):
    n = x.shape[0] // 4
    return (x[:n] * x[n : 2 * n]) * (x[2 * n : 3 * n] * x[3 * n :])


def pair_kernel(row_ref, qid_ref, queries_ref, passages_ref, basis_ref, sim_ref, held, arrived):
    groups = row_ref.shape[0] // GROUP
    query_len, feature_dim = queries_ref.shape[1:]
    length = held.shape[2]

    def fetch(group, u):
        half = lax.rem(group, 2)
        return pltpu.make_async_copy(
            passages_ref.at[row_ref[group * GROUP + u]], held.at[half, u], arrived.at[half, u]
        )

    for u in range(GROUP):
        fetch(0, u).start()

    @pl.loop(0, groups)
    def _(group):
        first = group * GROUP

        @pl.when(group + 1 < groups)
        def _():
            for u in range(GROUP):
                fetch(group + 1, u).start()

        for u in range(GROUP):
            fetch(group, u).wait()
        half = lax.rem(group, 2)
        pairs, scores = [], []
        for u in range(0, GROUP, 2):
            tile = held[half, u : u + 2].reshape(2 * length, feature_dim)
            stacked = jnp.concatenate(
                [queries_ref[qid_ref[first + u]], queries_ref[qid_ref[first + u + 1]]], axis=0
            )
            both = lax.dot_general(
                stacked, tile, (((1,), (1,)), ((), ())), preferred_element_type=jnp.float32
            )
            pairs.append(tile)
            scores += [both[:query_len, :length], both[query_len:, length:]]
        largest = [jnp.max(s, axis=1, keepdims=True) for s in scores]
        raised = [jnp.exp(s - m) for s, m in zip(scores, largest)]
        totals = [jnp.sum(r, axis=1, keepdims=True) for r in raised]
        guesses = [pl.reciprocal(t, approx=True) for t in totals]
        inverse = [g * (2.0 - t * g) for g, t in zip(guesses, totals)]
        weights = [(r * v).astype(jnp.bfloat16) for r, v in zip(raised, inverse)]
        blank = jnp.zeros((query_len, length), jnp.bfloat16)
        for u in range(0, GROUP, 2):
            spread = jnp.concatenate(
                [
                    jnp.concatenate([weights[u], blank], axis=1),
                    jnp.concatenate([blank, weights[u + 1]], axis=1),
                ],
                axis=0,
            )
            both = jnp.dot(spread, pairs[u // 2], preferred_element_type=jnp.float32)
            basis_ref[first + u] = both[:query_len].astype(jnp.bfloat16)
            basis_ref[first + u + 1] = both[query_len:].astype(jnp.bfloat16)
        rows = [
            jnp.sum(quarter_sum(m) + jnp.log(quarter_product(t)), axis=0, keepdims=True)
            for m, t in zip(largest, totals)
        ]
        sim_ref[pl.ds(pl.multiple_of(first, GROUP), GROUP), :] = jnp.broadcast_to(
            jnp.concatenate(rows, axis=0), (GROUP, sim_ref.shape[1])
        )


def pair_terms(rows, qids, queries, passages):
    slots = rows.shape[0]
    query_len, feature_dim = queries.shape[1:]
    return pl.pallas_call(
        pair_kernel,
        out_shape=(
            jax.ShapeDtypeStruct((slots, query_len, feature_dim), jnp.bfloat16),
            jax.ShapeDtypeStruct((slots, 128), jnp.float32),
        ),
        in_specs=[pl.BlockSpec(memory_space=pltpu.SMEM)] * 2
        + [pl.BlockSpec(memory_space=pltpu.VMEM), pl.BlockSpec(memory_space=pltpu.HBM)],
        out_specs=(pl.BlockSpec(memory_space=pltpu.VMEM),) * 2,
        scratch_shapes=[
            pltpu.VMEM((2, GROUP) + passages.shape[1:], passages.dtype),
            pltpu.SemaphoreType.DMA((2, GROUP)),
        ],
        compiler_params=pltpu.CompilerParams(vmem_limit_bytes=48 * 1024 * 1024),
    )(rows, qids, queries, passages)


def greet(shards, me):
    barrier = pltpu.get_barrier_semaphore()
    for step in range(1, shards):
        pl.semaphore_signal(
            barrier, inc=1, device_id={"bank": lax.rem(me + step, shards)}, device_id_type=MESH
        )
    pl.semaphore_wait(barrier, shards - 1)


def gather_kernel(shards, inner, q_ref, info_ref, all_q_ref, all_info_ref, sends, recvs, isends, irecvs):
    outer = shards // inner
    me = lax.axis_index("bank")
    z, y = me // inner, lax.rem(me, inner)
    rows = q_ref.shape[0]

    def place(index):
        return pl.ds(pl.multiple_of(index * rows, rows), rows)

    def peer(dz, dy):
        return lax.rem(z + dz, outer) * inner + lax.rem(y + dy, inner)

    def send(src, block, slot, target):
        copy = pltpu.make_async_remote_copy(
            src_ref=src,
            dst_ref=all_q_ref.at[place(block)],
            send_sem=sends.at[slot],
            recv_sem=recvs.at[slot],
            device_id={"bank": target},
            device_id_type=MESH,
        )
        copy.start()
        return copy

    greet(shards, me)
    copies = {}
    for dz in range(1, outer):
        copies[dz * inner] = send(q_ref, me, dz * inner, peer(dz, 0))
    small = []
    for step in range(1, shards):
        copy = pltpu.make_async_remote_copy(
            src_ref=info_ref,
            dst_ref=all_info_ref.at[place(me)],
            send_sem=isends.at[step],
            recv_sem=irecvs.at[step],
            device_id={"bank": lax.rem(me + step, shards)},
            device_id_type=MESH,
        )
        copy.start()
        small.append(copy)
    for dy in range(1, inner):
        copies[dy] = send(q_ref, me, dy, peer(0, dy))
    all_q_ref[place(me)] = q_ref[...]
    all_info_ref[place(me)] = info_ref[...]
    for dz in range(1, outer):
        copies[dz * inner].wait_recv()
        source = lax.rem(z + outer - dz, outer) * inner + y
        for dy in range(1, inner):
            copies[dz * inner + dy] = send(
                all_q_ref.at[place(source)], source, dz * inner + dy, peer(0, dy)
            )
    for slot, copy in copies.items():
        if slot < inner or slot % inner:
            copy.wait_recv()
        copy.wait_send()
    for copy in small:
        copy.wait()


def gather_queries(queries, info):
    shards = lax.axis_size("bank")
    inner = 1
    while (2 * inner) ** 2 <= shards:
        inner *= 2
    vmem = pl.BlockSpec(memory_space=pltpu.VMEM)
    return pl.pallas_call(
        functools.partial(gather_kernel, shards, inner),
        out_shape=(
            jax.ShapeDtypeStruct((shards * queries.shape[0],) + queries.shape[1:], queries.dtype),
            jax.ShapeDtypeStruct((shards * info.shape[0], info.shape[1]), info.dtype),
        ),
        in_specs=[vmem, vmem],
        out_specs=(vmem, vmem),
        scratch_shapes=[pltpu.SemaphoreType.DMA((shards,))] * 4,
        compiler_params=pltpu.CompilerParams(
            collective_id=0, has_side_effects=True, vmem_limit_bytes=16 * 1024 * 1024
        ),
    )(queries, info)


def contrast_kernel(shards, sim_ref, meta_ref, coef_ref, loss_ref, slots, sends, recvs):
    me = lax.axis_index("bank")
    width = coef_ref.shape[1]
    capacity = sim_ref.shape[0]
    meta = meta_ref[...]
    lane = lax.broadcasted_iota(jnp.int32, (capacity, width), 1)
    chosen = meta == lane * 2 + 1
    match = chosen | (meta == lane * 2)
    table = jnp.where(match, sim_ref[:, :1], -jnp.inf)
    largest = jnp.max(table, axis=0, keepdims=True)
    safe = jnp.where(largest == -jnp.inf, 0.0, largest)
    partial = jnp.sum(jnp.exp(table - safe), axis=0, keepdims=True)
    wanted = jnp.sum(jnp.where(chosen, table, 0.0), axis=0, keepdims=True)
    slots[me] = jnp.concatenate([largest, partial, wanted, jnp.zeros((5, width), jnp.float32)], axis=0)
    greet(shards, me)
    copies = []
    for step in range(1, shards):
        copy = pltpu.make_async_remote_copy(
            src_ref=slots.at[me],
            dst_ref=slots.at[me],
            send_sem=sends.at[step],
            recv_sem=recvs.at[step],
            device_id={"bank": lax.rem(me + step, shards)},
            device_id_type=MESH,
        )
        copy.start()
        copies.append(copy)
    for copy in copies:
        copy.wait()
    tops = [slots[b, 0:1, :] for b in range(shards)]
    top = functools.reduce(jnp.maximum, tops)
    top = jnp.where(top == -jnp.inf, 0.0, top)
    total = sum(slots[b, 1:2, :] * jnp.exp(tops[b] - top) for b in range(shards))
    picked = sum(slots[b, 2:3, :] for b in range(shards))
    loss_ref[...] = jnp.broadcast_to(top + jnp.log(total) - picked, loss_ref.shape)
    total = jnp.where(total == 0.0, 1.0, total)
    shares = jnp.exp(table - top) / total
    coef_ref[...] = (shares - jnp.where(chosen, 1.0, 0.0)).astype(coef_ref.dtype)


def contrast(sims, meta, group):
    shards = lax.axis_size("bank")
    width = -(-group // 128) * 128
    vmem = pl.BlockSpec(memory_space=pltpu.VMEM)
    return pl.pallas_call(
        functools.partial(contrast_kernel, shards),
        out_shape=(
            jax.ShapeDtypeStruct((sims.shape[0], width), jnp.bfloat16),
            jax.ShapeDtypeStruct((8, width), jnp.float32),
        ),
        in_specs=[vmem, vmem],
        out_specs=(vmem, vmem),
        scratch_shapes=[
            pltpu.VMEM((shards, 8, width), jnp.float32),
            pltpu.SemaphoreType.DMA((shards,)),
            pltpu.SemaphoreType.DMA((shards,)),
        ],
        compiler_params=pltpu.CompilerParams(
            collective_id=1, has_side_effects=True, vmem_limit_bytes=16 * 1024 * 1024
        ),
    )(sims, meta)


def slot_list(storage, positive, holdings, capacity):
    count, listed = storage.shape
    me = lax.axis_index("bank")
    owned = (storage // holdings == me).reshape(-1)
    entry = jnp.arange(count * listed, dtype=jnp.int32)
    picked = (jnp.arange(listed, dtype=jnp.int32)[None, :] == positive[:, None]).astype(jnp.int32)
    query = entry // listed
    code = (query * 2 + picked.reshape(-1)) * holdings + (storage % holdings).reshape(-1)
    position = jnp.cumsum(owned.astype(jnp.int32)) - 1
    target = jnp.where(owned, position, -1)
    here = target[None, :] == jnp.arange(capacity, dtype=jnp.int32)[:, None]
    table = jnp.sum(jnp.where(here, code[None, :] + 1, 0), axis=1) - 1
    meta = jnp.where(table >= 0, table // holdings, -1)
    table = jnp.maximum(table, 0)
    return table % holdings, table // holdings // 2, meta


def body(queries, passages, passage_home, candidates, positive):
    shards = lax.axis_size("bank")
    query_rows, query_len, feature_dim = queries.shape
    listed = candidates.shape[1]
    holdings = passages.shape[0]
    capacity = 3 * query_rows * listed
    group = shards * query_rows
    info = jnp.concatenate([passage_home[candidates], positive[:, None]], axis=1)
    info = jnp.pad(info, ((0, 0), (0, 128 - info.shape[1])))
    all_queries, infos = gather_queries(queries, info)
    rows, qids, meta = slot_list(infos[:, :listed], infos[:, listed], holdings, capacity)
    basis, sims = pair_terms(rows, qids, all_queries, passages)
    coefficients, losses = contrast(sims, meta[:, None], group)
    mine = lax.axis_index("bank") * query_rows
    losses = lax.dynamic_slice_in_dim(losses[0], mine, query_rows, 0)
    part = lax.dot_general(
        coefficients[:, :group],
        basis.reshape(capacity, query_len * feature_dim),
        (((0,), (0,)), ((), ())),
        preferred_element_type=jnp.float32,
    ).astype(jnp.bfloat16)
    parts = lax.all_to_all(
        part.reshape(shards, query_rows, query_len * feature_dim), "bank", 0, 0, tiled=True
    )
    gradient = jnp.sum(parts.astype(jnp.float32), axis=0)
    return (losses, gradient.reshape(query_rows, query_len, feature_dim))


def solution(mesh):
    return jax.shard_map(
        body,
        mesh=mesh,
        in_specs=(
            P(("query", "bank"), None, None),
            P("bank", None, None),
            P(),
            P(("query", "bank"), None),
            P(("query", "bank")),
        ),
        out_specs=(P(("query", "bank")), P(("query", "bank"), None, None)),
        check_vma=False,
    )
```
